32 devices in a mesh: fsdp: 4 (over y, x), ctx: 8 (over z, core).
Axes of the slice: x: 2, y: 2, z: 4, core: 2. Of those that a mesh axis runs over, the one named last changes fastest.
Arguments:
- tokens: bfloat16 [4, 8, 2, 64, 768], P('fsdp', 'ctx'), may hold values from -6 to 6
- cotangent: bfloat16 [4, 8, 2, 64, 768], P('fsdp', 'ctx'), may hold values from -6 to 6
- pair_of_rank: int32 [8], replicated, may hold values from 0 to 7, each once
- ln1_gain: bfloat16 [768], P('fsdp'), may hold values from 0.5 to 1.5
- ln1_shift: bfloat16 [768], P('fsdp'), may hold values from -4 to 4
- w_qkv: bfloat16 [768, 2304], P('fsdp'), may hold values from -0.21875 to 0.21875
- bias_q: bfloat16 [768], P('fsdp'), may hold values from -4 to 4
- bias_v: bfloat16 [768], P('fsdp'), may hold values from -4 to 4
- w_out: bfloat16 [768, 768], P('fsdp'), may hold values from -4 to 4
- bias_out: bfloat16 [768], P('fsdp'), may hold values from -4 to 4
- ln2_gain: bfloat16 [768], P('fsdp'), may hold values from 0.5 to 1.5
- ln2_shift: bfloat16 [768], P('fsdp'), may hold values from -4 to 4
- w_up: bfloat16 [768, 3072], P('fsdp'), may hold values from -0.21875 to 0.21875
- bias_up: bfloat16 [3072], P('fsdp'), may hold values from -4 to 4
- w_down: bfloat16 [3072, 768], P('fsdp'), may hold values from -0.109375 to 0.109375
- bias_down: bfloat16 [768], P('fsdp'), may hold values from -4 to 4
Outputs:
- layer_out: bfloat16 [4, 8, 2, 64, 768], P('fsdp', 'ctx')
- grad_tokens: bfloat16 [4, 8, 2, 64, 768], P('fsdp', 'ctx')
- grad_ln1_gain: float32 [768], P('fsdp')
- grad_ln1_shift: float32 [768], P('fsdp')
- grad_w_qkv: float32 [768, 2304], P('fsdp')
- grad_bias_q: float32 [768], P('fsdp')
- grad_bias_v: float32 [768], P('fsdp')
- grad_w_out: float32 [768, 768], P('fsdp')
- grad_bias_out: float32 [768], P('fsdp')
- grad_ln2_gain: float32 [768], P('fsdp')
- grad_ln2_shift: float32 [768], P('fsdp')
- grad_w_up: float32 [768, 3072], P('fsdp')
- grad_bias_up: float32 [3072], P('fsdp')
- grad_w_down: float32 [3072, 768], P('fsdp')
- grad_bias_down: float32 [768], P('fsdp')
The draws below stay inside these ranges and needn't reach their ends.
Inputs may be any that keep to these rules, and one draw needn't show every extreme that they name: `pair_of_rank`: each of 0 to 7 once.
All inputs are finite; a program needn't handle non-finite values.
Results may differ from the reference program's by a relative error of at most 0.018.
Values may be sent and summed in bfloat16 or wider, within the bound.
A program may use at most 128 MiB of HBM per device.

```python
import math
import jax
import jax.numpy as jnp
from jax import lax

D = 768
HEADS = 12
HDIM = 64
FF = 3072
BLK = 64
SEQS = 4
LEN = 1024
N_CTX = 8


def steps_of(rng, dims, split, least, high):
    factor_of, own = 1.0, jax.random.fold_in(rng, 6)
    for position, blocks in split:
        draws = jnp.exp(jax.random.uniform(jax.random.fold_in(own, position), (blocks,), jnp.float32, least / len(split), high / len(split)))
        factor_of = factor_of * jnp.repeat(draws, dims[position] // blocks).reshape([-1 if axis == position else 1 for axis in range(len(dims))])
    return factor_of


def bell_draw(rng, extent, scale, reach, split=(), held_as=jnp.bfloat16):
    values = jax.random.normal(rng, extent, jnp.float32) * scale
    if len(split) > 0:
        values = steps_of(rng, extent, split, -0.22, 0.18) * values
    return jnp.clip(values, min=-reach, max=reach).astype(held_as)


def setup_inputs(seed: int = 0) -> dict:
    arg_keys = jax.random.split(jax.random.key(seed), 17)
    tokens = bell_draw(arg_keys[0], (SEQS, N_CTX, 2, BLK, D), 1.0, 6.0, ((0, 4), (1, 8)))
    cotangent = bell_draw(arg_keys[1], (SEQS, N_CTX, 2, BLK, D), 1.0, 6.0, ((0, 4), (1, 8)))
    pair_of_rank = jax.random.permutation(arg_keys[2], N_CTX).astype(jnp.int32)
    ln1_gain = jnp.clip(1.0 + 0.1 * jax.random.normal(arg_keys[3], (D,), jnp.float32), 0.5, 1.5).astype(jnp.bfloat16)
    ln1_shift = bell_draw(arg_keys[4], (D,), 0.3, 4.0, ((0, 4),))
    w_qkv = bell_draw(arg_keys[5], (D, 3 * D), D ** -0.5, 0.21875, ((0, 4),))
    bias_q = bell_draw(arg_keys[6], (D,), 0.3, 4.0, ((0, 4),))
    bias_v = bell_draw(arg_keys[7], (D,), 0.3, 4.0, ((0, 4),))
    w_out = bell_draw(arg_keys[8], (D, D), (max(D // 384, 1)) ** -0.5, 4.0, ((0, 4),))
    bias_out = bell_draw(arg_keys[9], (D,), 0.3, 4.0, ((0, 4),))
    ln2_gain = jnp.clip(1.0 + 0.1 * jax.random.normal(arg_keys[10], (D,), jnp.float32), 0.5, 1.5).astype(jnp.bfloat16)
    ln2_shift = bell_draw(arg_keys[11], (D,), 0.3, 4.0, ((0, 4),))
    w_up = bell_draw(arg_keys[12], (D, FF), D ** -0.5, 0.21875, ((0, 4),))
    bias_up = bell_draw(arg_keys[13], (FF,), 0.3, 4.0, ((0, 4),))
    w_down = bell_draw(arg_keys[14], (FF, D), FF ** -0.5, 0.109375, ((0, 4),))
    bias_down = bell_draw(arg_keys[15], (D,), 0.3, 4.0, ((0, 4),))
    return {"tokens": tokens, "cotangent": cotangent, "pair_of_rank": pair_of_rank, "ln1_gain": ln1_gain, "ln1_shift": ln1_shift, "w_qkv": w_qkv, "bias_q": bias_q, "bias_v": bias_v, "w_out": w_out, "bias_out": bias_out, "ln2_gain": ln2_gain, "ln2_shift": ln2_shift, "w_up": w_up, "bias_up": bias_up, "w_down": w_down, "bias_down": bias_down}


@jax.custom_vjp
def low(v):
    return lax.optimization_barrier(v.astype(jnp.bfloat16)).astype(jnp.float32)

@jax.custom_vjp
def low_back(v):
    return v

def low_keep(v):
    return (low(v), None)

def low_pass(kept, grad):
    return (grad,)

def back_keep(v):
    return (v, None)

def back_low(kept, grad):
    return (low(grad),)
low.defvjp(low_keep, low_pass)
low_back.defvjp(back_keep, back_low)
EPS = 1e-05
MASKED = -1e+30
HIGH = lax.Precision.HIGHEST

def norm_rows(z, gain, shift):
    mean = lax.optimization_barrier(jnp.mean(z, axis=-1, keepdims=True))
    cent = z - mean
    var = lax.optimization_barrier(jnp.mean(cent * cent, axis=-1, keepdims=True))
    return cent * lax.rsqrt(var + EPS) * gain + shift

def attention(query, keys, values):
    qblock = math.gcd(512, LEN)
    scale = HDIM ** (-0.5)
    key_pos = jnp.arange(LEN, dtype=jnp.int32)

    def one_block(index):
        start = (index * qblock).astype(jnp.int32)
        qpart = lax.dynamic_slice_in_dim(query, start, qblock, 0)
        scores = jnp.einsum('qhe,khe->hqk', qpart, keys, precision=HIGH) * scale
        query_pos = start + jnp.arange(qblock, dtype=jnp.int32)
        visible = query_pos[:, None] >= key_pos[None, :]
        scores = low_back(jnp.where(visible[None], scores, MASKED))
        top = lax.optimization_barrier(jnp.max(scores, axis=-1, keepdims=True))
        expo = jnp.exp(scores - top)
        probs = low(expo / lax.optimization_barrier(jnp.sum(expo, axis=-1, keepdims=True)))
        return jnp.einsum('hqk,khe->qhe', probs, values, precision=HIGH).reshape(qblock, D)
    pieces = lax.map(jax.checkpoint(one_block), jnp.arange(LEN // qblock, dtype=jnp.int32))
    return pieces.reshape(LEN, D)

def layer(params, xseq):
    g1, s1, wqkv, bq, bv, wo, bo, g2, s2, wup, bup, wdown, bdown = params
    a1 = low(norm_rows(xseq, g1, s1))
    bias = jnp.concatenate([bq, jnp.zeros_like(bq), bv])
    qkv = low(low_back(jnp.dot(a1, wqkv, precision=HIGH) + bias))
    query = qkv[:, :D].reshape(LEN, HEADS, HDIM)
    keys = qkv[:, D:2 * D].reshape(LEN, HEADS, HDIM)
    values = qkv[:, 2 * D:].reshape(LEN, HEADS, HDIM)
    attn = low(low_back(attention(query, keys, values)))
    branch = low_back(jnp.dot(attn, wo, precision=HIGH) + bo)
    y1 = xseq + branch
    a2 = low(norm_rows(y1, g2, s2))
    upper = low_back(jnp.dot(a2, wup, precision=HIGH) + bup)
    act = low(jax.nn.gelu(upper))
    mlp = low_back(jnp.dot(act, wdown, precision=HIGH) + bdown)
    return y1 + mlp

def reference(tokens, cotangent, pair_of_rank, ln1_gain, ln1_shift, w_qkv, bias_q, bias_v, w_out, bias_out, ln2_gain, ln2_shift, w_up, bias_up, w_down, bias_down):
    ids = jnp.stack([pair_of_rank, 2 * N_CTX - 1 - pair_of_rank], axis=1).reshape(-1).astype(jnp.int32)

    def natural(arr):
        blocks = arr.astype(jnp.float32).reshape(SEQS, 2 * N_CTX, BLK, D)
        placed = jnp.zeros((SEQS, 2 * N_CTX, BLK, D), jnp.float32).at[:, ids].set(blocks)
        return placed.reshape(SEQS, LEN, D)

    def stored(arr):
        return arr.reshape(SEQS, 2 * N_CTX, BLK, D)[:, ids].reshape(SEQS, N_CTX, 2, BLK, D).astype(jnp.bfloat16)
    params = tuple((p.astype(jnp.float32) for p in (ln1_gain, ln1_shift, w_qkv, bias_q, bias_v, w_out, bias_out, ln2_gain, ln2_shift, w_up, bias_up, w_down, bias_down)))

    def step(acc, pair):
        xseq, gseq = pair
        yseq, pull = jax.vjp(layer, params, xseq)
        dparams, dx = pull(gseq)
        acc = jax.tree.map(lambda a, b: a + b, acc, dparams)
        return (acc, (yseq, dx))
    zeros = jax.tree.map(jnp.zeros_like, params)
    grads, (outs, dxs) = lax.scan(step, zeros, (natural(tokens), natural(cotangent)))
    return (stored(outs), stored(dxs), grads[0], grads[1], grads[2], grads[3], grads[4], grads[5], grads[6], grads[7], grads[8], grads[9], grads[10], grads[11], grads[12])
```

```python
import functools

import jax
import jax.numpy as jnp
from jax import lax
from jax.experimental import pallas as pl
from jax.experimental.pallas import tpu as pltpu
from jax.sharding import PartitionSpec as P

HDIM = 64
EPS = 1e-05
MASKED = -1e30
VMEM_LIMIT = 56 * 1024 * 1024
F32 = jnp.float32
BF16 = jnp.bfloat16


def norm_rows(z, gain, shift):
    mean = jnp.mean(z, axis=-1, keepdims=True)
    cent = z - mean
    var = jnp.mean(cent * cent, axis=-1, keepdims=True)
    return cent * lax.rsqrt(var + EPS) * gain + shift


def mm(a, b, ca, cb):
    return lax.dot_general(a, b, (((ca,), (cb,)), ((), ())), preferred_element_type=F32)


def head_pair(part, scale):
    lane = lax.broadcasted_iota(jnp.int32, part.shape, 1)
    part = (part.astype(F32) * scale).astype(part.dtype)
    zero = jnp.zeros_like(part)
    return jnp.concatenate(
        [jnp.where(lane < HDIM, part, zero), jnp.where(lane < HDIM, zero, part)], axis=0
    )


def join_pair(both):
    rows = both.shape[0] // 2
    lane = lax.broadcasted_iota(jnp.int32, (rows, both.shape[1]), 1)
    return jnp.where(lane < HDIM, both[:rows], both[rows:])


def mask_bias(qpos_ref, kpos_ref):
    seen = qpos_ref[...] >= kpos_ref[...]
    bias = jnp.where(seen, 0.0, MASKED)
    return jnp.concatenate([bias, bias], axis=0)


def attn_fwd_kernel(qkv_ref, kv_ref, qpos_ref, kpos_ref, out_ref, lse_ref, bias_ref):
    width = out_ref.shape[1]
    bias_ref[...] = mask_bias(qpos_ref, kpos_ref)
    for pair in range(width // 128):
        col = pair * 128
        query = head_pair(qkv_ref[:, col : col + 128], HDIM**-0.5)
        scores = mm(query, kv_ref[:, col : col + 128], 1, 1) + bias_ref[...]
        top = jnp.max(scores, axis=1, keepdims=True)
        expo = jnp.exp(scores - top)
        total = jnp.sum(expo, axis=1, keepdims=True)
        res = mm(expo.astype(BF16), kv_ref[:, width + col : width + col + 128], 1, 0)
        out_ref[:, col : col + 128] = join_pair(res / total).astype(BF16)
        lse_ref[:, pair : pair + 1] = top + jnp.log(total)


def attn_bwd_kernel(qkv_ref, kv_ref, do_ref, lse_ref, qpos_ref, kpos_ref, dq_ref, dkv_ref, bias_ref):
    width = dq_ref.shape[1]
    scale = HDIM**-0.5
    bias_ref[...] = mask_bias(qpos_ref, kpos_ref)
    for pair in range(width // 128):
        col = pair * 128
        query = head_pair(qkv_ref[:, col : col + 128], scale)
        d_out = head_pair(do_ref[:, col : col + 128], 1.0)
        keys = kv_ref[:, col : col + 128]
        scores = mm(query, keys, 1, 1) + bias_ref[...]
        probs = jnp.exp(scores - lse_ref[:, pair : pair + 1])
        dkv_ref[:, width + col : width + col + 128] = mm(probs.astype(BF16), d_out, 0, 0).astype(BF16)
        d_probs = mm(d_out, kv_ref[:, width + col : width + col + 128], 1, 1)
        delta = jnp.sum(probs * d_probs, axis=1, keepdims=True)
        d_scores = (probs * (d_probs - delta)).astype(BF16)
        dq_ref[:, col : col + 128] = (join_pair(mm(d_scores, keys, 1, 0)) * scale).astype(BF16)
        dkv_ref[:, col : col + 128] = mm(d_scores, query, 0, 0).astype(BF16)


def attn_fwd(qkv, kv, qpos, kpos):
    rows, width, span = qkv.shape[0], qkv.shape[1] // 3, kv.shape[0]
    return pl.pallas_call(
        attn_fwd_kernel,
        out_shape=(
            jax.ShapeDtypeStruct((rows, width), BF16),
            jax.ShapeDtypeStruct((2 * rows, 128), F32),
        ),
        scratch_shapes=[pltpu.VMEM((2 * rows, span), F32)],
        compiler_params=pltpu.CompilerParams(vmem_limit_bytes=VMEM_LIMIT),
        name="attn_fwd",
    )(qkv, kv, qpos, kpos)


def attn_bwd(qkv, kv, d_out, lse, qpos, kpos):
    rows, width, span = qkv.shape[0], qkv.shape[1] // 3, kv.shape[0]
    return pl.pallas_call(
        attn_bwd_kernel,
        out_shape=(
            jax.ShapeDtypeStruct((rows, width), BF16),
            jax.ShapeDtypeStruct((span, 2 * width), BF16),
        ),
        scratch_shapes=[pltpu.VMEM((2 * rows, span), F32)],
        compiler_params=pltpu.CompilerParams(vmem_limit_bytes=VMEM_LIMIT),
        name="attn_bwd",
    )(qkv, kv, d_out, lse, qpos, kpos)


class PlainComm:

    def gather(self, *arrays):
        return [lax.all_gather(a, "fsdp", axis=0, tiled=True) for a in arrays]

    def gather_attn(self, w_qkv, w_out, small):
        return self.gather(w_qkv, w_out, small[None])

    def gather_mlp(self, qkv, w_up, w_down):
        kv = lax.all_gather(qkv[:, qkv.shape[1] // 3 :], "ctx", axis=0, tiled=True)
        return kv, *self.gather(w_up, w_down)

    def reduce(self, *arrays):
        return [
            lax.psum(lax.psum_scatter(a, "fsdp", scatter_dimension=0, tiled=True), "ctx")
            for a in arrays
        ]

    def reduce_mlp(self, d_kv, g_wup, g_wdown):
        own = lax.psum_scatter(d_kv, "ctx", scatter_dimension=0, tiled=True)
        return own, *self.reduce(g_wup, g_wdown)

    def reduce_attn(self, g_wqkv, g_wout, g_small):
        s_wqkv, s_wout, s_small = self.reduce(g_wqkv, g_wout, g_small)
        return s_wqkv, s_wout, s_small.reshape(-1)


def body(
    tokens, cotangent, pair_of_rank, ln1_gain, ln1_shift, w_qkv, bias_q, bias_v, w_out, bias_out,
    ln2_gain, ln2_shift, w_up, bias_up, w_down, bias_down, *, comm
):
    blk, width = tokens.shape[3], tokens.shape[4]
    shards = lax.axis_size("fsdp")
    parts = lax.axis_size("ctx")
    rank = lax.axis_index("ctx")
    rows = tokens.shape[0] * 2 * blk
    span = parts * 2 * blk
    ff = w_up.shape[1]
    each = ln1_gain.shape[0]

    small = jnp.concatenate(
        [ln1_gain, ln1_shift, bias_q, bias_v, bias_out, ln2_gain, ln2_shift, bias_down, bias_up]
    )
    wqkv_all, wout_all, small_all = comm.gather_attn(w_qkv, w_out, small)
    small_all = small_all.astype(F32)
    vec = lambda i: small_all[:, i * each : (i + 1) * each].reshape(width)
    gain1, shift1, bq_all, bv_all, bout_all, gain2, shift2, bdown_all = (vec(i) for i in range(8))
    bup_all = small_all[:, 8 * each :].reshape(ff)

    inputs = tokens.reshape(rows, width).astype(F32)
    a_one = norm_rows(inputs, gain1, shift1).astype(BF16)
    qkv_bias = jnp.concatenate([bq_all, jnp.zeros((width,), F32), bv_all])
    qkv = (mm(a_one, wqkv_all, 1, 0) + qkv_bias).astype(BF16)
    kv, wup_all, wdown_all = comm.gather_mlp(qkv, w_up, w_down)

    own = pair_of_rank[rank]
    offsets = jnp.arange(blk, dtype=jnp.int32)
    qpos = jnp.concatenate([own * blk + offsets, (2 * parts - 1 - own) * blk + offsets])[:, None]
    key_blocks = jnp.stack([pair_of_rank, 2 * parts - 1 - pair_of_rank], axis=1)
    kpos = (key_blocks[:, :, None] * blk + offsets[None, None, :]).reshape(1, span)

    mixed, lse = attn_fwd(qkv, kv, qpos, kpos)
    resid = inputs + mm(mixed, wout_all, 1, 0) + bout_all
    a_two = norm_rows(resid, gain2, shift2).astype(BF16)
    upper = mm(a_two, wup_all, 1, 0) + bup_all
    active, gelu_pull = jax.vjp(jax.nn.gelu, upper)
    a_three = active.astype(BF16)
    layer_out = (resid + mm(a_three, wdown_all, 1, 0) + bdown_all).astype(BF16).reshape(tokens.shape)

    d_mlp = cotangent.reshape(rows, width)
    grad_rows = d_mlp.astype(F32)
    g_bdown = jnp.sum(grad_rows, axis=0)
    g_wdown = mm(a_three, d_mlp, 0, 0).astype(BF16)
    d_upper = gelu_pull(mm(d_mlp, wdown_all, 1, 1))[0].astype(BF16)
    g_bup = jnp.sum(d_upper.astype(F32), axis=0)
    g_wup = mm(a_two, d_upper, 0, 0).astype(BF16)
    d_htwo = mm(d_upper, wup_all, 1, 1)
    d_resid_norm, g_gain2, g_shift2 = jax.vjp(norm_rows, resid, gain2, shift2)[1](d_htwo)
    d_resid = grad_rows + d_resid_norm
    d_branch = d_resid.astype(BF16)
    g_bout = jnp.sum(d_branch.astype(F32), axis=0)
    g_wout = mm(mixed, d_branch, 0, 0).astype(BF16)
    d_mixed = mm(d_branch, wout_all, 1, 1).astype(BF16)

    d_query, d_kv_all = attn_bwd(qkv, kv, d_mixed, lse, qpos, kpos)
    d_kv, s_wup, s_wdown = comm.reduce_mlp(d_kv_all, g_wup, g_wdown)
    d_qkv = jnp.concatenate([d_query, d_kv], axis=1)
    g_bq = jnp.sum(d_query.astype(F32), axis=0)
    g_bv = jnp.sum(d_kv[:, width:].astype(F32), axis=0)
    g_wqkv = mm(a_one, d_qkv, 0, 0).astype(BF16)
    d_hone = mm(d_qkv, wqkv_all, 1, 1)
    d_input_norm, g_gain1, g_shift1 = jax.vjp(norm_rows, inputs, gain1, shift1)[1](d_hone)
    grad_tokens = (d_resid + d_input_norm).astype(BF16).reshape(tokens.shape)

    cut = lambda g: g.reshape(shards, -1)
    g_small = jnp.concatenate(
        [cut(g) for g in (g_gain1, g_shift1, g_bq, g_bv, g_bout, g_gain2, g_shift2, g_bdown, g_bup)],
        axis=1,
    ).astype(BF16)
    s_wqkv, s_wout, s_small = comm.reduce_attn(g_wqkv, g_wout, g_small)
    s_small = s_small.astype(F32)
    s_gain1, s_shift1, s_bq, s_bv, s_bout, s_gain2, s_shift2, s_bdown = (
        s_small[i * each : (i + 1) * each] for i in range(8)
    )
    s_bup = s_small[8 * each :]
    return (
        layer_out, grad_tokens, s_gain1, s_shift1, s_wqkv.astype(F32), s_bq, s_bv, s_wout.astype(F32),
        s_bout, s_gain2, s_shift2, s_wup.astype(F32), s_bup, s_wdown.astype(F32), s_bdown,
    )


def solution(mesh):
    split = P("fsdp", "ctx", None, None, None)
    row, mat = P("fsdp"), P("fsdp", None)
    in_specs = (
        split, split, P(), row, row, mat, row, row, mat, row, row, row, mat, row, mat, row,
    )
    out_specs = (
        split, split, row, row, mat, row, row, mat, row, row, row, mat, row, mat, row,
    )
    comm = PlainComm()
    return jax.shard_map(
        functools.partial(body, comm=comm),
        mesh=mesh, in_specs=in_specs, out_specs=out_specs, check_vma=False,
    )
```

```python
import functools

import jax
import jax.numpy as jnp
from jax import lax
from jax.experimental import pallas as pl
from jax.experimental.pallas import tpu as pltpu
from jax.sharding import PartitionSpec as P

HDIM = 64
EPS = 1e-05
MASKED = -1e30
VMEM_LIMIT = 56 * 1024 * 1024
F32 = jnp.float32
BF16 = jnp.bfloat16
MESH = pl.DeviceIdType.MESH


def norm_rows(z, gain, shift):
    mean = jnp.mean(z, axis=-1, keepdims=True)
    cent = z - mean
    var = jnp.mean(cent * cent, axis=-1, keepdims=True)
    return cent * lax.rsqrt(var + EPS) * gain + shift


def mm(a, b, ca, cb):
    return lax.dot_general(a, b, (((ca,), (cb,)), ((), ())), preferred_element_type=F32)


def head_pair(part, scale):
    lane = lax.broadcasted_iota(jnp.int32, part.shape, 1)
    part = (part.astype(F32) * scale).astype(part.dtype)
    zero = jnp.zeros_like(part)
    return jnp.concatenate(
        [jnp.where(lane < HDIM, part, zero), jnp.where(lane < HDIM, zero, part)], axis=0
    )


def join_pair(both):
    rows = both.shape[0] // 2
    lane = lax.broadcasted_iota(jnp.int32, (rows, both.shape[1]), 1)
    return jnp.where(lane < HDIM, both[:rows], both[rows:])


def mask_bias(qpos_ref, kpos_ref):
    seen = qpos_ref[...] >= kpos_ref[...]
    bias = jnp.where(seen, 0.0, MASKED)
    return jnp.concatenate([bias, bias], axis=0)


def attn_fwd_kernel(qkv_ref, kv_ref, qpos_ref, kpos_ref, out_ref, lse_ref, bias_ref):
    width = out_ref.shape[1]
    bias_ref[...] = mask_bias(qpos_ref, kpos_ref)
    for pair in range(width // 128):
        col = pair * 128
        query = head_pair(qkv_ref[:, col : col + 128], HDIM**-0.5)
        scores = mm(query, kv_ref[:, col : col + 128], 1, 1) + bias_ref[...]
        top = jnp.max(scores, axis=1, keepdims=True)
        expo = jnp.exp(scores - top)
        total = jnp.sum(expo, axis=1, keepdims=True)
        res = mm(expo.astype(BF16), kv_ref[:, width + col : width + col + 128], 1, 0)
        out_ref[:, col : col + 128] = join_pair(res / total).astype(BF16)
        lse_ref[:, pair : pair + 1] = top + jnp.log(total)


def attn_bwd_kernel(qkv_ref, kv_ref, do_ref, lse_ref, qpos_ref, kpos_ref, dq_ref, dkv_ref, bias_ref):
    width = dq_ref.shape[1]
    scale = HDIM**-0.5
    bias_ref[...] = mask_bias(qpos_ref, kpos_ref)
    for pair in range(width // 128):
        col = pair * 128
        query = head_pair(qkv_ref[:, col : col + 128], scale)
        d_out = head_pair(do_ref[:, col : col + 128], 1.0)
        keys = kv_ref[:, col : col + 128]
        scores = mm(query, keys, 1, 1) + bias_ref[...]
        probs = jnp.exp(scores - lse_ref[:, pair : pair + 1])
        dkv_ref[:, width + col : width + col + 128] = mm(probs.astype(BF16), d_out, 0, 0).astype(BF16)
        d_probs = mm(d_out, kv_ref[:, width + col : width + col + 128], 1, 1)
        delta = jnp.sum(probs * d_probs, axis=1, keepdims=True)
        d_scores = (probs * (d_probs - delta)).astype(BF16)
        dq_ref[:, col : col + 128] = (join_pair(mm(d_scores, keys, 1, 0)) * scale).astype(BF16)
        dkv_ref[:, col : col + 128] = mm(d_scores, query, 0, 0).astype(BF16)


def attn_fwd(qkv, kv, qpos, kpos):
    rows, width, span = qkv.shape[0], qkv.shape[1] // 3, kv.shape[0]
    return pl.pallas_call(
        attn_fwd_kernel,
        out_shape=(
            jax.ShapeDtypeStruct((rows, width), BF16),
            jax.ShapeDtypeStruct((2 * rows, 128), F32),
        ),
        scratch_shapes=[pltpu.VMEM((2 * rows, span), F32)],
        compiler_params=pltpu.CompilerParams(vmem_limit_bytes=VMEM_LIMIT),
        name="attn_fwd",
    )(qkv, kv, qpos, kpos)


def attn_bwd(qkv, kv, d_out, lse, qpos, kpos):
    rows, width, span = qkv.shape[0], qkv.shape[1] // 3, kv.shape[0]
    return pl.pallas_call(
        attn_bwd_kernel,
        out_shape=(
            jax.ShapeDtypeStruct((rows, width), BF16),
            jax.ShapeDtypeStruct((span, 2 * width), BF16),
        ),
        scratch_shapes=[pltpu.VMEM((2 * rows, span), F32)],
        compiler_params=pltpu.CompilerParams(vmem_limit_bytes=VMEM_LIMIT),
        name="attn_bwd",
    )(qkv, kv, d_out, lse, qpos, kpos)


class PlainComm:

    def gather(self, *arrays):
        return [lax.all_gather(a, "fsdp", axis=0, tiled=True) for a in arrays]

    def gather_attn(self, w_qkv, w_out, small):
        return self.gather(w_qkv, w_out, small[None])

    def gather_mlp(self, qkv, w_up, w_down):
        kv = lax.all_gather(qkv[:, qkv.shape[1] // 3 :], "ctx", axis=0, tiled=True)
        return kv, *self.gather(w_up, w_down)

    def reduce(self, *arrays):
        return [
            lax.psum(lax.psum_scatter(a, "fsdp", scatter_dimension=0, tiled=True), "ctx")
            for a in arrays
        ]

    def reduce_mlp(self, d_kv, g_wup, g_wdown):
        own = lax.psum_scatter(d_kv, "ctx", scatter_dimension=0, tiled=True)
        return own, *self.reduce(g_wup, g_wdown)

    def reduce_attn(self, g_wqkv, g_wout, g_small):
        s_wqkv, s_wout, s_small = self.reduce(g_wqkv, g_wout, g_small)
        return s_wqkv, s_wout, s_small.reshape(-1)


class Place:

    def __init__(self):
        self.f = lax.axis_index("fsdp")
        self.c = lax.axis_index("ctx")
        self.nz = lax.axis_size("ctx") // 2
        self.z = lax.div(self.c, 2)
        self.core = lax.rem(self.c, 2)
        self.fx = self.f + 1 - 2 * lax.rem(self.f, 2)
        self.fy = lax.rem(self.f + 2, 4)
        self.fd = lax.rem(self.fx + 2, 4)
        self.x_dev = (self.fx, self.c)
        self.y_dev = (self.fy, self.c)
        self.sib_dev = (self.f, self.c + 1 - 2 * self.core)

    def z_ahead(self, k):
        return lax.rem(self.z + k, self.nz)

    def z_behind(self, k):
        return lax.rem(self.z + self.nz - k, self.nz)

    def z_dev(self, z):
        return (self.f, 2 * z + self.core)

    def greet(self, along_z):
        partners = [self.x_dev, self.y_dev, self.sib_dev]
        if along_z:
            partners += [self.z_dev(self.z_ahead(k)) for k in range(1, self.nz)]
        barrier = pltpu.get_barrier_semaphore()
        for dev in partners:
            pl.semaphore_signal(barrier, inc=1, device_id=dev, device_id_type=MESH)
        pl.semaphore_wait(barrier, len(partners))


def at(start, size, unit):
    return pl.ds(pl.multiple_of(start, unit), size)


def send(src, dst, sems, row, idx, dev):
    copy = pltpu.make_async_remote_copy(
        src_ref=src, dst_ref=dst, send_sem=sems[0].at[row, idx], recv_sem=sems[1].at[row, idx],
        device_id=dev, device_id_type=MESH,
    )
    copy.start()
    return copy


def gather_kernel(count, with_kv, *refs):
    place = Place()
    n_in = count + with_kv
    shards, outs = refs[:count], refs[n_in : n_in + count]
    rest = refs[2 * n_in :]
    sems, local = rest[:2], rest[2]
    place.greet(with_kv)
    started, stay = [], []

    def piece(i, src, sub):
        rows, cols = shards[i].shape
        half, wide = rows // 2, cols // 2
        return outs[i].at[at(src * rows + sub * half, half, 16), at(place.core * wide, wide, 128)]

    first, second, third = [], [], []
    for i in range(count):
        rows, cols = shards[i].shape
        half, wide = rows // 2, cols // 2
        mine = [
            shards[i].at[pl.ds(sub * half, half), at(place.core * wide, wide, 128)] for sub in (0, 1)
        ]
        to = [piece(i, place.f, sub) for sub in (0, 1)]
        xa = send(mine[0], to[0], sems, i, 0, place.x_dev)
        yb = send(mine[1], to[1], sems, i, 3, place.y_dev)
        xb = send(mine[1], to[1], sems, i, 1, place.x_dev)
        ya = send(mine[0], to[0], sems, i, 2, place.y_dev)
        first.append((i, xa, yb, xb, ya))
        own = pltpu.make_async_copy(
            shards[i], outs[i].at[at(place.f * rows, rows, 16), :], local.at[i]
        )
        own.start()
        stay.append(own)

    if with_kv:
        qkv, kv_out = refs[count], refs[n_in + count]
        rows, cols = kv_out.shape[0] // (2 * place.nz), kv_out.shape[1]
        block = qkv.at[:, pl.ds(qkv.shape[1] - cols, cols)]
        spot = lambda c: kv_out.at[at(c * rows, rows, 16), :]
        kv_moves = [
            send(block, spot(place.c), sems, count, k, place.z_dev(place.z_ahead(k)))
            for k in range(1, place.nz)
        ]
        started += [send(block, spot(place.c), sems, count, 0, place.sib_dev)]
        own = pltpu.make_async_copy(block, spot(place.c), local.at[count])
        own.start()
        stay.append(own)

    def pass_on(i, src, sub, idx):
        ref = piece(i, src, sub)
        return send(ref, ref, sems, i, idx, place.sib_dev)

    for i, xa, yb, xb, ya in first:
        xa.wait_recv()
        ref = piece(i, place.fx, 0)
        fa = send(ref, ref, sems, i, 4, place.y_dev)
        yb.wait_recv()
        ref = piece(i, place.fy, 1)
        fb = send(ref, ref, sems, i, 5, place.x_dev)
        second.append((i, fa, fb))
        started += [pass_on(i, place.fx, 0, 6), pass_on(i, place.fy, 1, 7)]
        xb.wait_recv()
        ya.wait_recv()
        started += [pass_on(i, place.fx, 1, 8), pass_on(i, place.fy, 0, 9)]
        third += [xa, yb, xb, ya]
    if with_kv:
        for k in range(1, place.nz):
            kv_moves[k - 1].wait_recv()
            ref = spot(2 * place.z_behind(k) + place.core)
            started.append(send(ref, ref, sems, count, place.nz + k, place.sib_dev))
        third += kv_moves
    for i, fa, fb in second:
        fa.wait_recv()
        fb.wait_recv()
        started += [pass_on(i, place.fd, 0, 10), pass_on(i, place.fd, 1, 11)]
        third += [fa, fb]
    for copy in third:
        copy.wait_send()
    for copy in started:
        copy.wait()
    for copy in stay:
        copy.wait()


def gather_call(arrays, qkv, number):
    count, with_kv = len(arrays), int(qkv is not None)
    shards, parts = lax.axis_size("fsdp"), lax.axis_size("ctx")
    out = [jax.ShapeDtypeStruct((shards * a.shape[0], a.shape[1]), BF16) for a in arrays]
    args = list(arrays)
    if with_kv:
        args.append(qkv)
        out.append(jax.ShapeDtypeStruct((parts * qkv.shape[0], qkv.shape[1] // 3 * 2), BF16))
    sems = pltpu.SemaphoreType.DMA((count + with_kv, 12))
    return pl.pallas_call(
        functools.partial(gather_kernel, count, with_kv),
        out_shape=tuple(out),
        in_specs=[pl.BlockSpec(memory_space=pl.ANY)] * len(args),
        out_specs=(pl.BlockSpec(memory_space=pl.ANY),) * len(out),
        scratch_shapes=[sems, sems, pltpu.SemaphoreType.DMA((count + with_kv,))],
        compiler_params=pltpu.CompilerParams(
            collective_id=number, has_side_effects=True, vmem_limit_bytes=VMEM_LIMIT
        ),
        name="gather_%d" % number,
    )(*args)


def chunk_width(rows, half):
    for wide in (384, 256, 128):
        if half % wide == 0 and (rows * wide <= 768 * 384 or wide == 128):
            return wide


def reduce_kernel(count, with_kv, *refs):
    place = Place()
    nz = place.nz
    n_in = count + with_kv
    grads, outs = refs[:count], refs[n_in : n_in + count]
    rest = list(refs[2 * n_in :])
    sems = (rest.pop(0), rest.pop(0))
    bufs = [[rest.pop(0) for _ in range(7)] for _ in range(count)]
    place.greet(True)
    moves, ends = [], []
    add = lambda *terms: sum(t.astype(F32) for t in terms).astype(BF16)

    jobs = []
    for i in range(count):
        rows, half = grads[i].shape[0] // 4, grads[i].shape[1] // 2
        wide = chunk_width(4 * rows, half)
        jobs += [(i, off, wide) for off in range(0, half, wide)]

    class Job:
        pass

    work = []
    if with_kv:
        d_kv, kv_out = refs[count], refs[n_in + count]
        kv_sib, kv_sum, kv_got = rest[:3]
        kv_sems = (rest[3], rest[4])
        rows = kv_out.shape[0]
        block = lambda c: d_kv.at[at(c * rows, rows, 16), :]
        to_sib = []
        for k in [*range(1, nz), 0]:
            dest = place.z_ahead(k)
            to_sib.append(
                send(block(2 * dest + 1 - place.core), kv_sib.at[k], kv_sems, 0, k, place.sib_dev)
            )
    for row, (i, off, wide) in enumerate(jobs):
        job = Job()
        job.row, job.i, job.wide = row, i, wide
        job.rows, job.half = grads[i].shape[0] // 4, grads[i].shape[1] // 2
        job.cols = pl.ds(off, wide)
        job.mine = at(place.core * job.half + off, wide, 128)
        job.his = at((1 - place.core) * job.half + off, wide, 128)
        job.g, job.out = grads[i], outs[i]
        job.sib, job.cs, job.one, job.mid, job.two, job.zs, job.zb = bufs[i]
        job.m0 = send(job.g.at[:, job.his], job.sib.at[:, job.cols], sems, row, 0, place.sib_dev)
        moves.append(job.m0)
        work.append(job)
    if with_kv:
        kv_moves = []
        for k, got in zip([*range(1, nz), 0], to_sib):
            got.wait_recv()
            dest = place.z_ahead(k)
            kv_sum[k] = add(block(2 * dest + place.core)[...], kv_sib[k])
            if k:
                kv_moves.append(
                    send(kv_sum.at[k], kv_got.at[k - 1], kv_sems, 0, nz + k, place.z_dev(dest))
                )
        moves += to_sib + kv_moves

    def rows_of(job, who, sub):
        half = job.rows // 2
        return at(who * job.rows + sub * half, half, 16)

    def stage_one(job):
        job.m0.wait_recv()
        job.cs[:, job.cols] = add(job.g[:, job.mine], job.sib[:, job.cols])
        cut = lambda who, sub: job.cs.at[rows_of(job, who, sub), job.cols]
        spot = lambda n: job.one.at[n, :, job.cols]
        job.m1 = [
            send(cut(place.fd, 0), spot(1), sems, job.row, 2, place.y_dev),
            send(cut(place.fd, 1), spot(3), sems, job.row, 4, place.x_dev),
            send(cut(place.fy, 0), spot(0), sems, job.row, 1, place.y_dev),
            send(cut(place.fx, 1), spot(2), sems, job.row, 3, place.x_dev),
        ]
        moves.extend(job.m1)

    def stage_two(job):
        for move in job.m1[:2]:
            move.wait_recv()
        job.mid[0, :, job.cols] = add(
            job.cs[rows_of(job, place.fx, 0), job.cols], job.one[1, :, job.cols]
        )
        job.mid[1, :, job.cols] = add(
            job.cs[rows_of(job, place.fy, 1), job.cols], job.one[3, :, job.cols]
        )
        job.m2 = [
            send(
                job.mid.at[n, :, job.cols], job.two.at[n, :, job.cols], sems, job.row, 5 + n, dev
            )
            for n, dev in ((0, place.x_dev), (1, place.y_dev))
        ]
        moves.extend(job.m2)

    def stage_three(job):
        for move in job.m1[2:] + job.m2:
            move.wait_recv()
        half, quarter = job.rows // 2, job.rows // nz
        for n in (0, 1):
            job.zs[pl.ds(n * half, half), job.cols] = add(
                job.cs[rows_of(job, place.f, n), job.cols],
                job.one[2 * n, :, job.cols],
                job.two[n, :, job.cols],
            )
        job.m3 = []
        for k in range(1, nz):
            dest = place.z_ahead(k)
            job.m3.append(
                send(
                    job.zs.at[at(dest * quarter, quarter, 16), job.cols],
                    job.zb.at[k - 1, :, job.cols],
                    sems, job.row, 6 + k, place.z_dev(dest),
                )
            )
        moves.extend(job.m3)

    def own_rows(job, z):
        quarter = job.rows // nz
        return at(z * quarter, quarter, 16)

    def stage_four(job):
        for move in job.m3:
            move.wait_recv()
        mine = own_rows(job, place.z)
        job.out[mine, job.mine] = add(
            job.zs[mine, job.cols], *(job.zb[k, :, job.cols] for k in range(nz - 1))
        )
        ref = job.out.at[mine, job.mine]
        job.m4 = [
            send(ref, ref, sems, job.row, 5 + nz + k, place.z_dev(place.z_ahead(k)))
            for k in range(1, nz)
        ]
        moves.extend(job.m4)
        ends.append(send(ref, ref, sems, job.row, 5 + 2 * nz, place.sib_dev))

    def stage_five(job):
        for k, move in enumerate(job.m4, 1):
            move.wait_recv()
            ref = job.out.at[own_rows(job, place.z_behind(k)), job.mine]
            ends.append(send(ref, ref, sems, job.row, 5 + 2 * nz + k, place.sib_dev))

    stages = ((0, stage_one), (2, stage_two), (3, stage_three), (4, stage_four), (5, stage_five))
    for step in range(len(work) + 5):
        for lag, stage in stages:
            if 0 <= step - lag < len(work):
                stage(work[step - lag])
    if with_kv:
        for move in kv_moves:
            move.wait_recv()
        kv_out[...] = add(kv_sum[0], *(kv_got[k] for k in range(nz - 1)))
    for move in moves:
        move.wait_send()
    for move in ends:
        move.wait()


def reduce_call(arrays, d_kv, number):
    count, with_kv = len(arrays), int(d_kv is not None)
    nz = lax.axis_size("ctx") // 2
    out = [jax.ShapeDtypeStruct((a.shape[0] // 4, a.shape[1]), BF16) for a in arrays]
    args, scratch, jobs = list(arrays), [], 0
    for a in arrays:
        rows, half = a.shape[0] // 4, a.shape[1] // 2
        jobs += half // chunk_width(a.shape[0], half)
        scratch += [
            pltpu.VMEM(shape, BF16)
            for shape in (
                (4 * rows, half), (4 * rows, half), (4, rows // 2, half), (2, rows // 2, half),
                (2, rows // 2, half), (rows, half), (nz - 1, rows // nz, half),
            )
        ]
    sems = pltpu.SemaphoreType.DMA((jobs, 5 + 3 * nz))
    scratch = [sems, sems] + scratch
    if with_kv:
        args.append(d_kv)
        rows, cols = d_kv.shape[0] // (2 * nz), d_kv.shape[1]
        out.append(jax.ShapeDtypeStruct((rows, cols), BF16))
        kv_sems = pltpu.SemaphoreType.DMA((1, 2 * nz))
        scratch += [pltpu.VMEM((nz, rows, cols), BF16)] * 2
        scratch += [pltpu.VMEM((nz - 1, rows, cols), BF16), kv_sems, kv_sems]
    return pl.pallas_call(
        functools.partial(reduce_kernel, count, with_kv),
        out_shape=tuple(out),
        in_specs=[pl.BlockSpec(memory_space=pltpu.VMEM)] * len(args),
        out_specs=(pl.BlockSpec(memory_space=pltpu.VMEM),) * len(out),
        scratch_shapes=scratch,
        compiler_params=pltpu.CompilerParams(
            collective_id=number, has_side_effects=True, vmem_limit_bytes=VMEM_LIMIT
        ),
        name="reduce_%d" % number,
    )(*args)


class ChipComm:

    def gather_attn(self, w_qkv, w_out, small):
        size = small.shape[0]
        packed = jnp.pad(small, (0, 32 * 256 - size)).reshape(32, 256)
        wqkv_all, wout_all, small_all = gather_call([w_qkv, w_out, packed], None, 1)
        return wqkv_all, wout_all, small_all.reshape(-1, 32 * 256)[:, :size]

    def gather_mlp(self, qkv, w_up, w_down):
        wup_all, wdown_all, kv = gather_call([w_up, w_down], qkv, 2)
        return kv, wup_all, wdown_all

    def reduce_mlp(self, d_kv, g_wup, g_wdown):
        s_wup, s_wdown, own = reduce_call([g_wup, g_wdown], d_kv, 3)
        return own, s_wup, s_wdown

    def reduce_attn(self, g_wqkv, g_wout, g_small):
        size = g_small.shape[1]
        packed = jnp.pad(g_small, ((0, 0), (0, 64 * 256 - size))).reshape(-1, 256)
        s_wqkv, s_wout, s_small = reduce_call([g_wqkv, g_wout, packed], None, 4)
        return s_wqkv, s_wout, s_small.reshape(-1)[:size]


def has_chips(mesh):
    return mesh.shape["fsdp"] == 4 and mesh.shape["ctx"] == 8


def body(
    tokens, cotangent, pair_of_rank, ln1_gain, ln1_shift, w_qkv, bias_q, bias_v, w_out, bias_out,
    ln2_gain, ln2_shift, w_up, bias_up, w_down, bias_down, *, comm
):
    blk, width = tokens.shape[3], tokens.shape[4]
    shards = lax.axis_size("fsdp")
    parts = lax.axis_size("ctx")
    rank = lax.axis_index("ctx")
    rows = tokens.shape[0] * 2 * blk
    span = parts * 2 * blk
    ff = w_up.shape[1]
    each = ln1_gain.shape[0]

    small = jnp.concatenate(
        [ln1_gain, ln1_shift, bias_q, bias_v, bias_out, ln2_gain, ln2_shift, bias_down, bias_up]
    )
    wqkv_all, wout_all, small_all = comm.gather_attn(w_qkv, w_out, small)
    small_all = small_all.astype(F32)
    vec = lambda i: small_all[:, i * each : (i + 1) * each].reshape(width)
    gain1, shift1, bq_all, bv_all, bout_all, gain2, shift2, bdown_all = (vec(i) for i in range(8))
    bup_all = small_all[:, 8 * each :].reshape(ff)

    inputs = tokens.reshape(rows, width).astype(F32)
    a_one = norm_rows(inputs, gain1, shift1).astype(BF16)
    qkv_bias = jnp.concatenate([bq_all, jnp.zeros((width,), F32), bv_all])
    qkv = (mm(a_one, wqkv_all, 1, 0) + qkv_bias).astype(BF16)
    kv, wup_all, wdown_all = comm.gather_mlp(qkv, w_up, w_down)

    own = pair_of_rank[rank]
    offsets = jnp.arange(blk, dtype=jnp.int32)
    qpos = jnp.concatenate([own * blk + offsets, (2 * parts - 1 - own) * blk + offsets])[:, None]
    key_blocks = jnp.stack([pair_of_rank, 2 * parts - 1 - pair_of_rank], axis=1)
    kpos = (key_blocks[:, :, None] * blk + offsets[None, None, :]).reshape(1, span)

    mixed, lse = attn_fwd(qkv, kv, qpos, kpos)
    resid = inputs + mm(mixed, wout_all, 1, 0) + bout_all
    a_two = norm_rows(resid, gain2, shift2).astype(BF16)
    upper = mm(a_two, wup_all, 1, 0) + bup_all
    active, gelu_pull = jax.vjp(jax.nn.gelu, upper)
    a_three = active.astype(BF16)
    layer_out = (resid + mm(a_three, wdown_all, 1, 0) + bdown_all).astype(BF16).reshape(tokens.shape)

    d_mlp = cotangent.reshape(rows, width)
    grad_rows = d_mlp.astype(F32)
    g_bdown = jnp.sum(grad_rows, axis=0)
    g_wdown = mm(a_three, d_mlp, 0, 0).astype(BF16)
    d_upper = gelu_pull(mm(d_mlp, wdown_all, 1, 1))[0].astype(BF16)
    g_bup = jnp.sum(d_upper.astype(F32), axis=0)
    g_wup = mm(a_two, d_upper, 0, 0).astype(BF16)
    d_htwo = mm(d_upper, wup_all, 1, 1)
    d_resid_norm, g_gain2, g_shift2 = jax.vjp(norm_rows, resid, gain2, shift2)[1](d_htwo)
    d_resid = grad_rows + d_resid_norm
    d_branch = d_resid.astype(BF16)
    g_bout = jnp.sum(d_branch.astype(F32), axis=0)
    g_wout = mm(mixed, d_branch, 0, 0).astype(BF16)
    d_mixed = mm(d_branch, wout_all, 1, 1).astype(BF16)

    d_query, d_kv_all = attn_bwd(qkv, kv, d_mixed, lse, qpos, kpos)
    d_kv, s_wup, s_wdown = comm.reduce_mlp(d_kv_all, g_wup, g_wdown)
    d_qkv = jnp.concatenate([d_query, d_kv], axis=1)
    g_bq = jnp.sum(d_query.astype(F32), axis=0)
    g_bv = jnp.sum(d_kv[:, width:].astype(F32), axis=0)
    g_wqkv = mm(a_one, d_qkv, 0, 0).astype(BF16)
    d_hone = mm(d_qkv, wqkv_all, 1, 1)
    d_input_norm, g_gain1, g_shift1 = jax.vjp(norm_rows, inputs, gain1, shift1)[1](d_hone)
    grad_tokens = (d_resid + d_input_norm).astype(BF16).reshape(tokens.shape)

    cut = lambda g: g.reshape(shards, -1)
    g_small = jnp.concatenate(
        [cut(g) for g in (g_gain1, g_shift1, g_bq, g_bv, g_bout, g_gain2, g_shift2, g_bdown, g_bup)],
        axis=1,
    ).astype(BF16)
    s_wqkv, s_wout, s_small = comm.reduce_attn(g_wqkv, g_wout, g_small)
    s_small = s_small.astype(F32)
    s_gain1, s_shift1, s_bq, s_bv, s_bout, s_gain2, s_shift2, s_bdown = (
        s_small[i * each : (i + 1) * each] for i in range(8)
    )
    s_bup = s_small[8 * each :]
    return (
        layer_out, grad_tokens, s_gain1, s_shift1, s_wqkv.astype(F32), s_bq, s_bv, s_wout.astype(F32),
        s_bout, s_gain2, s_shift2, s_wup.astype(F32), s_bup, s_wdown.astype(F32), s_bdown,
    )


def solution(mesh):
    split = P("fsdp", "ctx", None, None, None)
    row, mat = P("fsdp"), P("fsdp", None)
    in_specs = (
        split, split, P(), row, row, mat, row, row, mat, row, row, row, mat, row, mat, row,
    )
    out_specs = (
        split, split, row, row, mat, row, row, mat, row, row, row, mat, row, mat, row,
    )
    comm = ChipComm() if has_chips(mesh) else PlainComm()
    return jax.shard_map(
        functools.partial(body, comm=comm),
        mesh=mesh, in_specs=in_specs, out_specs=out_specs, check_vma=False,
    )
```

```python
import functools

import jax
import jax.numpy as jnp
from jax import lax
from jax.experimental import pallas as pl
from jax.experimental.pallas import tpu as pltpu
from jax.sharding import PartitionSpec as P

HDIM = 64
EPS = 1e-05
MASKED = -1e30
VMEM_LIMIT = 56 * 1024 * 1024
F32 = jnp.float32
BF16 = jnp.bfloat16
MESH = pl.DeviceIdType.MESH


def norm_rows(z, gain, shift):
    mean = jnp.mean(z, axis=-1, keepdims=True)
    cent = z - mean
    var = jnp.mean(cent * cent, axis=-1, keepdims=True)
    return cent * lax.rsqrt(var + EPS) * gain + shift


def mm(a, b, ca, cb):
    return lax.dot_general(a, b, (((ca,), (cb,)), ((), ())), preferred_element_type=F32)


def head_pair(part, scale):
    lane = lax.broadcasted_iota(jnp.int32, part.shape, 1)
    part = (part.astype(F32) * scale).astype(part.dtype)
    zero = jnp.zeros_like(part)
    return jnp.concatenate(
        [jnp.where(lane < HDIM, part, zero), jnp.where(lane < HDIM, zero, part)], axis=0
    )


def join_pair(both):
    rows = both.shape[0] // 2
    lane = lax.broadcasted_iota(jnp.int32, (rows, both.shape[1]), 1)
    return jnp.where(lane < HDIM, both[:rows], both[rows:])


def mask_bias(qpos_ref, kpos_ref):
    seen = qpos_ref[...] >= kpos_ref[...]
    bias = jnp.where(seen, 0.0, MASKED)
    return jnp.concatenate([bias, bias], axis=0)


def attn_fwd_kernel(qkv_ref, kv_ref, qpos_ref, kpos_ref, out_ref, lse_ref, bias_ref):
    width = out_ref.shape[1]
    bias_ref[...] = mask_bias(qpos_ref, kpos_ref)
    for pair in range(width // 128):
        col = pair * 128
        query = head_pair(qkv_ref[:, col : col + 128], HDIM**-0.5)
        scores = mm(query, kv_ref[:, col : col + 128], 1, 1) + bias_ref[...]
        top = jnp.max(scores, axis=1, keepdims=True)
        expo = jnp.exp(scores - top)
        total = jnp.sum(expo, axis=1, keepdims=True)
        res = mm(expo.astype(BF16), kv_ref[:, width + col : width + col + 128], 1, 0)
        out_ref[:, col : col + 128] = join_pair(res / total).astype(BF16)
        lse_ref[:, pair : pair + 1] = top + jnp.log(total)


def attn_bwd_kernel(qkv_ref, kv_ref, do_ref, lse_ref, qpos_ref, kpos_ref, dq_ref, dkv_ref, bias_ref):
    width = dq_ref.shape[1]
    scale = HDIM**-0.5
    bias_ref[...] = mask_bias(qpos_ref, kpos_ref)
    for pair in range(width // 128):
        col = pair * 128
        query = head_pair(qkv_ref[:, col : col + 128], scale)
        d_out = head_pair(do_ref[:, col : col + 128], 1.0)
        keys = kv_ref[:, col : col + 128]
        scores = mm(query, keys, 1, 1) + bias_ref[...]
        probs = jnp.exp(scores - lse_ref[:, pair : pair + 1])
        dkv_ref[:, width + col : width + col + 128] = mm(probs.astype(BF16), d_out, 0, 0).astype(BF16)
        d_probs = mm(d_out, kv_ref[:, width + col : width + col + 128], 1, 1)
        delta = jnp.sum(probs * d_probs, axis=1, keepdims=True)
        d_scores = (probs * (d_probs - delta)).astype(BF16)
        dq_ref[:, col : col + 128] = (join_pair(mm(d_scores, keys, 1, 0)) * scale).astype(BF16)
        dkv_ref[:, col : col + 128] = mm(d_scores, query, 0, 0).astype(BF16)


def attn_fwd(qkv, kv, qpos, kpos):
    rows, width, span = qkv.shape[0], qkv.shape[1] // 3, kv.shape[0]
    return pl.pallas_call(
        attn_fwd_kernel,
        out_shape=(
            jax.ShapeDtypeStruct((rows, width), BF16),
            jax.ShapeDtypeStruct((2 * rows, 128), F32),
        ),
        scratch_shapes=[pltpu.VMEM((2 * rows, span), F32)],
        compiler_params=pltpu.CompilerParams(vmem_limit_bytes=VMEM_LIMIT),
        name="attn_fwd",
    )(qkv, kv, qpos, kpos)


def attn_bwd(qkv, kv, d_out, lse, qpos, kpos):
    rows, width, span = qkv.shape[0], qkv.shape[1] // 3, kv.shape[0]
    return pl.pallas_call(
        attn_bwd_kernel,
        out_shape=(
            jax.ShapeDtypeStruct((rows, width), BF16),
            jax.ShapeDtypeStruct((span, 2 * width), BF16),
        ),
        scratch_shapes=[pltpu.VMEM((2 * rows, span), F32)],
        compiler_params=pltpu.CompilerParams(vmem_limit_bytes=VMEM_LIMIT),
        name="attn_bwd",
    )(qkv, kv, d_out, lse, qpos, kpos)


class PlainComm:

    def gather(self, *arrays):
        return [lax.all_gather(a, "fsdp", axis=0, tiled=True) for a in arrays]

    def gather_attn(self, w_qkv, w_out, small):
        return self.gather(w_qkv, w_out, small[None])

    def gather_mlp(self, qkv, w_up, w_down):
        kv = lax.all_gather(qkv[:, qkv.shape[1] // 3 :], "ctx", axis=0, tiled=True)
        return kv, *self.gather(w_up, w_down)

    def reduce(self, *arrays):
        return [
            lax.psum(lax.psum_scatter(a, "fsdp", scatter_dimension=0, tiled=True), "ctx")
            for a in arrays
        ]

    def reduce_mlp(self, d_kv, g_wup, g_wdown):
        own = lax.psum_scatter(d_kv, "ctx", scatter_dimension=0, tiled=True)
        return own, *self.reduce(g_wup, g_wdown)

    def reduce_attn(self, g_wqkv, g_wout, g_small):
        s_wqkv, s_wout, s_small = self.reduce(g_wqkv, g_wout, g_small)
        return s_wqkv, s_wout, s_small.reshape(-1)


class Place:

    def __init__(self):
        self.f = lax.axis_index("fsdp")
        self.c = lax.axis_index("ctx")
        self.nz = lax.axis_size("ctx") // 2
        self.z = lax.div(self.c, 2)
        self.core = lax.rem(self.c, 2)
        self.fx = self.f + 1 - 2 * lax.rem(self.f, 2)
        self.fy = lax.rem(self.f + 2, 4)
        self.fd = lax.rem(self.fx + 2, 4)
        self.x_dev = (self.fx, self.c)
        self.y_dev = (self.fy, self.c)
        self.sib_dev = (self.f, self.c + 1 - 2 * self.core)

    def z_ahead(self, k):
        return lax.rem(self.z + k, self.nz)

    def z_behind(self, k):
        return lax.rem(self.z + self.nz - k, self.nz)

    def z_dev(self, z):
        return (self.f, 2 * z + self.core)

    def greet(self, along_z):
        partners = [self.x_dev, self.y_dev, self.sib_dev]
        if along_z:
            partners += [self.z_dev(self.z_ahead(k)) for k in range(1, self.nz)]
        barrier = pltpu.get_barrier_semaphore()
        for dev in partners:
            pl.semaphore_signal(barrier, inc=1, device_id=dev, device_id_type=MESH)
        pl.semaphore_wait(barrier, len(partners))


def at(start, size, unit):
    return pl.ds(pl.multiple_of(start, unit), size)


def send(src, dst, sems, row, idx, dev):
    copy = pltpu.make_async_remote_copy(
        src_ref=src, dst_ref=dst, send_sem=sems[0].at[row, idx], recv_sem=sems[1].at[row, idx],
        device_id=dev, device_id_type=MESH,
    )
    copy.start()
    return copy


def gather_kernel(count, with_kv, *refs):
    place = Place()
    n_in = count + with_kv
    shards, outs = refs[:count], refs[n_in : n_in + count]
    rest = refs[2 * n_in :]
    sems, local, held = rest[:2], rest[2], rest[3:]
    place.greet(with_kv)
    started, stay = [], []

    def stage_in(i, src, dst):
        copy = pltpu.make_async_copy(src, held[i], local.at[i, 0])
        copy.start()
        stay.append((copy, pltpu.make_async_copy(held[i], dst, local.at[i, 1])))

    def piece(i, src, sub):
        rows = shards[i].shape[0]
        part = rows // 4
        return outs[i].at[at(src * rows + (2 * place.core + sub) * part, part, 16), :]

    first, second, third = [], [], []
    for i in range(count):
        rows = shards[i].shape[0]
        part = rows // 4
        mine = [shards[i].at[at((2 * place.core + sub) * part, part, 16), :] for sub in (0, 1)]
        to = [piece(i, place.f, sub) for sub in (0, 1)]
        xa = send(mine[0], to[0], sems, i, 0, place.x_dev)
        yb = send(mine[1], to[1], sems, i, 3, place.y_dev)
        xb = send(mine[1], to[1], sems, i, 1, place.x_dev)
        ya = send(mine[0], to[0], sems, i, 2, place.y_dev)
        first.append((i, xa, yb, xb, ya))
        stage_in(i, shards[i], outs[i].at[at(place.f * rows, rows, 16), :])

    if with_kv:
        qkv, kv_out = refs[count], refs[n_in + count]
        rows, cols = kv_out.shape[0] // (2 * place.nz), kv_out.shape[1]
        block = qkv.at[:, pl.ds(qkv.shape[1] - cols, cols)]
        spot = lambda c: kv_out.at[at(c * rows, rows, 16), :]
        kv_moves = [
            send(block, spot(place.c), sems, count, k, place.z_dev(place.z_ahead(k)))
            for k in range(1, place.nz)
        ]
        started += [send(block, spot(place.c), sems, count, 0, place.sib_dev)]
        stage_in(count, block, spot(place.c))

    for copy_in, copy_out in stay:
        copy_in.wait()
        copy_out.start()

    def pass_on(i, src, sub, idx):
        ref = piece(i, src, sub)
        return send(ref, ref, sems, i, idx, place.sib_dev)

    for i, xa, yb, xb, ya in first:
        xa.wait_recv()
        ref = piece(i, place.fx, 0)
        fa = send(ref, ref, sems, i, 4, place.y_dev)
        yb.wait_recv()
        ref = piece(i, place.fy, 1)
        fb = send(ref, ref, sems, i, 5, place.x_dev)
        second.append((i, fa, fb))
        started += [pass_on(i, place.fx, 0, 6), pass_on(i, place.fy, 1, 7)]
        xb.wait_recv()
        ya.wait_recv()
        started += [pass_on(i, place.fx, 1, 8), pass_on(i, place.fy, 0, 9)]
        third += [xa, yb, xb, ya]
    if with_kv:
        for k in range(1, place.nz):
            kv_moves[k - 1].wait_recv()
            ref = spot(2 * place.z_behind(k) + place.core)
            started.append(send(ref, ref, sems, count, place.nz + k, place.sib_dev))
        third += kv_moves
    for i, fa, fb in second:
        fa.wait_recv()
        fb.wait_recv()
        started += [pass_on(i, place.fd, 0, 10), pass_on(i, place.fd, 1, 11)]
        third += [fa, fb]
    for copy in third:
        copy.wait_send()
    for copy in started:
        copy.wait()
    for _, copy_out in stay:
        copy_out.wait()


def gather_call(arrays, qkv, number):
    count, with_kv = len(arrays), int(qkv is not None)
    shards, parts = lax.axis_size("fsdp"), lax.axis_size("ctx")
    out = [jax.ShapeDtypeStruct((shards * a.shape[0], a.shape[1]), BF16) for a in arrays]
    args = list(arrays)
    if with_kv:
        args.append(qkv)
        out.append(jax.ShapeDtypeStruct((parts * qkv.shape[0], qkv.shape[1] // 3 * 2), BF16))
    sems = pltpu.SemaphoreType.DMA((count + with_kv, 12))
    held = [pltpu.VMEM(a.shape, BF16) for a in arrays]
    if with_kv:
        held.append(pltpu.VMEM((qkv.shape[0], out[-1].shape[1]), BF16))
    return pl.pallas_call(
        functools.partial(gather_kernel, count, with_kv),
        out_shape=tuple(out),
        in_specs=[pl.BlockSpec(memory_space=pl.ANY)] * len(args),
        out_specs=(pl.BlockSpec(memory_space=pl.ANY),) * len(out),
        scratch_shapes=[sems, sems, pltpu.SemaphoreType.DMA((count + with_kv, 2))] + held,
        compiler_params=pltpu.CompilerParams(
            collective_id=number, has_side_effects=True, vmem_limit_bytes=VMEM_LIMIT
        ),
        name="gather_%d" % number,
    )(*args)


def chunk_width(rows, half):
    for wide in (384, 256, 128):
        if half % wide == 0 and (rows * wide <= 768 * 384 or wide == 128):
            return wide


def reduce_kernel(count, with_kv, *refs):
    place = Place()
    nz = place.nz
    n_in = count + with_kv
    grads, outs = refs[:count], refs[n_in : n_in + count]
    rest = list(refs[2 * n_in :])
    sems = (rest.pop(0), rest.pop(0))
    bufs = [[rest.pop(0) for _ in range(7)] for _ in range(count)]
    place.greet(True)
    moves, ends = [], []
    add = lambda *terms: sum(t.astype(F32) for t in terms).astype(BF16)

    jobs = []
    for i in range(count):
        rows, half = grads[i].shape[0] // 4, grads[i].shape[1] // 2
        wide = chunk_width(4 * rows, half)
        jobs += [(i, off, wide) for off in range(0, half, wide)]

    class Job:
        pass

    work = []
    if with_kv:
        d_kv, kv_out = refs[count], refs[n_in + count]
        kv_sib, kv_sum, kv_got = rest[:3]
        kv_sems = (rest[3], rest[4])
        rows = kv_out.shape[0]
        block = lambda c: d_kv.at[at(c * rows, rows, 16), :]
        to_sib = []
        for k in [*range(1, nz), 0]:
            dest = place.z_ahead(k)
            to_sib.append(
                send(block(2 * dest + 1 - place.core), kv_sib.at[k], kv_sems, 0, k, place.sib_dev)
            )
    for row, (i, off, wide) in enumerate(jobs):
        job = Job()
        job.row, job.i, job.wide = row, i, wide
        job.rows, job.half = grads[i].shape[0] // 4, grads[i].shape[1] // 2
        job.cols = pl.ds(off, wide)
        job.mine = at(place.core * job.half + off, wide, 128)
        job.his = at((1 - place.core) * job.half + off, wide, 128)
        job.g, job.out = grads[i], outs[i]
        job.sib, job.cs, job.one, job.mid, job.two, job.zs, job.zb = bufs[i]
        job.m0 = send(job.g.at[:, job.his], job.sib.at[:, job.cols], sems, row, 0, place.sib_dev)
        moves.append(job.m0)
        work.append(job)
    if with_kv:
        kv_moves = []
        for k, got in zip([*range(1, nz), 0], to_sib):
            got.wait_recv()
            dest = place.z_ahead(k)
            kv_sum[k] = add(block(2 * dest + place.core)[...], kv_sib[k])
            if k:
                kv_moves.append(
                    send(kv_sum.at[k], kv_got.at[k - 1], kv_sems, 0, nz + k, place.z_dev(dest))
                )
        moves += to_sib + kv_moves

    def rows_of(job, who, sub):
        half = job.rows // 2
        return at(who * job.rows + sub * half, half, 16)

    def stage_one(job):
        job.m0.wait_recv()
        job.cs[:, job.cols] = add(job.g[:, job.mine], job.sib[:, job.cols])
        cut = lambda who, sub: job.cs.at[rows_of(job, who, sub), job.cols]
        spot = lambda n: job.one.at[n, :, job.cols]
        job.m1 = [
            send(cut(place.fd, 0), spot(1), sems, job.row, 2, place.y_dev),
            send(cut(place.fd, 1), spot(3), sems, job.row, 4, place.x_dev),
            send(cut(place.fy, 0), spot(0), sems, job.row, 1, place.y_dev),
            send(cut(place.fx, 1), spot(2), sems, job.row, 3, place.x_dev),
        ]
        moves.extend(job.m1)

    def stage_two(job):
        for move in job.m1[:2]:
            move.wait_recv()
        job.mid[0, :, job.cols] = add(
            job.cs[rows_of(job, place.fx, 0), job.cols], job.one[1, :, job.cols]
        )
        job.mid[1, :, job.cols] = add(
            job.cs[rows_of(job, place.fy, 1), job.cols], job.one[3, :, job.cols]
        )
        job.m2 = [
            send(
                job.mid.at[n, :, job.cols], job.two.at[n, :, job.cols], sems, job.row, 5 + n, dev
            )
            for n, dev in ((0, place.x_dev), (1, place.y_dev))
        ]
        moves.extend(job.m2)

    def stage_three(job):
        for move in job.m1[2:] + job.m2:
            move.wait_recv()
        half, quarter = job.rows // 2, job.rows // nz
        for n in (0, 1):
            job.zs[pl.ds(n * half, half), job.cols] = add(
                job.cs[rows_of(job, place.f, n), job.cols],
                job.one[2 * n, :, job.cols],
                job.two[n, :, job.cols],
            )
        job.m3 = []
        for k in range(1, nz):
            dest = place.z_ahead(k)
            job.m3.append(
                send(
                    job.zs.at[at(dest * quarter, quarter, 16), job.cols],
                    job.zb.at[k - 1, :, job.cols],
                    sems, job.row, 6 + k, place.z_dev(dest),
                )
            )
        moves.extend(job.m3)

    def own_rows(job, z):
        quarter = job.rows // nz
        return at(z * quarter, quarter, 16)

    def stage_four(job):
        for move in job.m3:
            move.wait_recv()
        mine = own_rows(job, place.z)
        job.out[mine, job.mine] = add(
            job.zs[mine, job.cols], *(job.zb[k, :, job.cols] for k in range(nz - 1))
        )
        ref = job.out.at[mine, job.mine]
        job.m4 = [
            send(ref, ref, sems, job.row, 5 + nz + k, place.z_dev(place.z_ahead(k)))
            for k in range(1, nz)
        ]
        moves.extend(job.m4)
        ends.append(send(ref, ref, sems, job.row, 5 + 2 * nz, place.sib_dev))

    def stage_five(job):
        for k, move in enumerate(job.m4, 1):
            move.wait_recv()
            ref = job.out.at[own_rows(job, place.z_behind(k)), job.mine]
            ends.append(send(ref, ref, sems, job.row, 5 + 2 * nz + k, place.sib_dev))

    stages = ((0, stage_one), (2, stage_two), (3, stage_three), (4, stage_four), (5, stage_five))
    for step in range(len(work) + 5):
        for lag, stage in stages:
            if 0 <= step - lag < len(work):
                stage(work[step - lag])
    if with_kv:
        for move in kv_moves:
            move.wait_recv()
        kv_out[...] = add(kv_sum[0], *(kv_got[k] for k in range(nz - 1)))
    for move in moves:
        move.wait_send()
    for move in ends:
        move.wait()


def reduce_call(arrays, d_kv, number):
    count, with_kv = len(arrays), int(d_kv is not None)
    nz = lax.axis_size("ctx") // 2
    out = [jax.ShapeDtypeStruct((a.shape[0] // 4, a.shape[1]), BF16) for a in arrays]
    args, scratch, jobs = list(arrays), [], 0
    for a in arrays:
        rows, half = a.shape[0] // 4, a.shape[1] // 2
        jobs += half // chunk_width(a.shape[0], half)
        scratch += [
            pltpu.VMEM(shape, BF16)
            for shape in (
                (4 * rows, half), (4 * rows, half), (4, rows // 2, half), (2, rows // 2, half),
                (2, rows // 2, half), (rows, half), (nz - 1, rows // nz, half),
            )
        ]
    sems = pltpu.SemaphoreType.DMA((jobs, 5 + 3 * nz))
    scratch = [sems, sems] + scratch
    if with_kv:
        args.append(d_kv)
        rows, cols = d_kv.shape[0] // (2 * nz), d_kv.shape[1]
        out.append(jax.ShapeDtypeStruct((rows, cols), BF16))
        kv_sems = pltpu.SemaphoreType.DMA((1, 2 * nz))
        scratch += [pltpu.VMEM((nz, rows, cols), BF16)] * 2
        scratch += [pltpu.VMEM((nz - 1, rows, cols), BF16), kv_sems, kv_sems]
    return pl.pallas_call(
        functools.partial(reduce_kernel, count, with_kv),
        out_shape=tuple(out),
        in_specs=[pl.BlockSpec(memory_space=pltpu.VMEM)] * len(args),
        out_specs=(pl.BlockSpec(memory_space=pltpu.VMEM),) * len(out),
        scratch_shapes=scratch,
        compiler_params=pltpu.CompilerParams(
            collective_id=number, has_side_effects=True, vmem_limit_bytes=VMEM_LIMIT
        ),
        name="reduce_%d" % number,
    )(*args)


class ChipComm:

    def gather_attn(self, w_qkv, w_out, small):
        size = small.shape[0]
        packed = jnp.pad(small, (0, 64 * 128 - size)).reshape(64, 128)
        wqkv_all, wout_all, small_all = gather_call([w_qkv, w_out, packed], None, 1)
        return wqkv_all, wout_all, small_all.reshape(-1, 64 * 128)[:, :size]

    def gather_mlp(self, qkv, w_up, w_down):
        wup_all, wdown_all, kv = gather_call([w_up, w_down], qkv, 2)
        return kv, wup_all, wdown_all

    def reduce_mlp(self, d_kv, g_wup, g_wdown):
        s_wup, s_wdown, own = reduce_call([g_wup, g_wdown], d_kv, 3)
        return own, s_wup, s_wdown

    def reduce_attn(self, g_wqkv, g_wout, g_small):
        size = g_small.shape[1]
        packed = jnp.pad(g_small, ((0, 0), (0, 64 * 256 - size))).reshape(-1, 256)
        s_wqkv, s_wout, s_small = reduce_call([g_wqkv, g_wout, packed], None, 4)
        return s_wqkv, s_wout, s_small.reshape(-1)[:size]


def has_chips(mesh):
    return mesh.shape["fsdp"] == 4 and mesh.shape["ctx"] == 8


def body(
    tokens, cotangent, pair_of_rank, ln1_gain, ln1_shift, w_qkv, bias_q, bias_v, w_out, bias_out,
    ln2_gain, ln2_shift, w_up, bias_up, w_down, bias_down, *, comm
):
    blk, width = tokens.shape[3], tokens.shape[4]
    shards = lax.axis_size("fsdp")
    parts = lax.axis_size("ctx")
    rank = lax.axis_index("ctx")
    rows = tokens.shape[0] * 2 * blk
    span = parts * 2 * blk
    ff = w_up.shape[1]
    each = ln1_gain.shape[0]

    small = jnp.concatenate(
        [ln1_gain, ln1_shift, bias_q, bias_v, bias_out, ln2_gain, ln2_shift, bias_down, bias_up]
    )
    wqkv_all, wout_all, small_all = comm.gather_attn(w_qkv, w_out, small)
    small_all = small_all.astype(F32)
    vec = lambda i: small_all[:, i * each : (i + 1) * each].reshape(width)
    gain1, shift1, bq_all, bv_all, bout_all, gain2, shift2, bdown_all = (vec(i) for i in range(8))
    bup_all = small_all[:, 8 * each :].reshape(ff)

    inputs = tokens.reshape(rows, width).astype(F32)
    a_one = norm_rows(inputs, gain1, shift1).astype(BF16)
    qkv_bias = jnp.concatenate([bq_all, jnp.zeros((width,), F32), bv_all])
    qkv = (mm(a_one, wqkv_all, 1, 0) + qkv_bias).astype(BF16)
    kv, wup_all, wdown_all = comm.gather_mlp(qkv, w_up, w_down)

    own = pair_of_rank[rank]
    offsets = jnp.arange(blk, dtype=jnp.int32)
    qpos = jnp.concatenate([own * blk + offsets, (2 * parts - 1 - own) * blk + offsets])[:, None]
    key_blocks = jnp.stack([pair_of_rank, 2 * parts - 1 - pair_of_rank], axis=1)
    kpos = (key_blocks[:, :, None] * blk + offsets[None, None, :]).reshape(1, span)

    mixed, lse = attn_fwd(qkv, kv, qpos, kpos)
    resid = inputs + mm(mixed, wout_all, 1, 0) + bout_all
    a_two = norm_rows(resid, gain2, shift2).astype(BF16)
    upper = mm(a_two, wup_all, 1, 0) + bup_all
    active, gelu_pull = jax.vjp(jax.nn.gelu, upper)
    a_three = active.astype(BF16)
    layer_out = (resid + mm(a_three, wdown_all, 1, 0) + bdown_all).astype(BF16).reshape(tokens.shape)

    d_mlp = cotangent.reshape(rows, width)
    grad_rows = d_mlp.astype(F32)
    g_bdown = jnp.sum(grad_rows, axis=0)
    g_wdown = mm(a_three, d_mlp, 0, 0).astype(BF16)
    d_upper = gelu_pull(mm(d_mlp, wdown_all, 1, 1))[0].astype(BF16)
    g_bup = jnp.sum(d_upper.astype(F32), axis=0)
    g_wup = mm(a_two, d_upper, 0, 0).astype(BF16)
    d_htwo = mm(d_upper, wup_all, 1, 1)
    d_resid_norm, g_gain2, g_shift2 = jax.vjp(norm_rows, resid, gain2, shift2)[1](d_htwo)
    d_resid = grad_rows + d_resid_norm
    d_branch = d_resid.astype(BF16)
    g_bout = jnp.sum(d_branch.astype(F32), axis=0)
    g_wout = mm(mixed, d_branch, 0, 0).astype(BF16)
    d_mixed = mm(d_branch, wout_all, 1, 1).astype(BF16)

    d_query, d_kv_all = attn_bwd(qkv, kv, d_mixed, lse, qpos, kpos)
    d_kv, s_wup, s_wdown = comm.reduce_mlp(d_kv_all, g_wup, g_wdown)
    d_qkv = jnp.concatenate([d_query, d_kv], axis=1)
    g_bq = jnp.sum(d_query.astype(F32), axis=0)
    g_bv = jnp.sum(d_kv[:, width:].astype(F32), axis=0)
    g_wqkv = mm(a_one, d_qkv, 0, 0).astype(BF16)
    d_hone = mm(d_qkv, wqkv_all, 1, 1)
    d_input_norm, g_gain1, g_shift1 = jax.vjp(norm_rows, inputs, gain1, shift1)[1](d_hone)
    grad_tokens = (d_resid + d_input_norm).astype(BF16).reshape(tokens.shape)

    cut = lambda g: g.reshape(shards, -1)
    g_small = jnp.concatenate(
        [cut(g) for g in (g_gain1, g_shift1, g_bq, g_bv, g_bout, g_gain2, g_shift2, g_bdown, g_bup)],
        axis=1,
    ).astype(BF16)
    s_wqkv, s_wout, s_small = comm.reduce_attn(g_wqkv, g_wout, g_small)
    s_small = s_small.astype(F32)
    s_gain1, s_shift1, s_bq, s_bv, s_bout, s_gain2, s_shift2, s_bdown = (
        s_small[i * each : (i + 1) * each] for i in range(8)
    )
    s_bup = s_small[8 * each :]
    return (
        layer_out, grad_tokens, s_gain1, s_shift1, s_wqkv.astype(F32), s_bq, s_bv, s_wout.astype(F32),
        s_bout, s_gain2, s_shift2, s_wup.astype(F32), s_bup, s_wdown.astype(F32), s_bdown,
    )


def solution(mesh):
    split = P("fsdp", "ctx", None, None, None)
    row, mat = P("fsdp"), P("fsdp", None)
    in_specs = (
        split, split, P(), row, row, mat, row, row, mat, row, row, row, mat, row, mat, row,
    )
    out_specs = (
        split, split, row, row, mat, row, row, mat, row, row, row, mat, row, mat, row,
    )
    comm = ChipComm() if has_chips(mesh) else PlainComm()
    return jax.shard_map(
        functools.partial(body, comm=comm),
        mesh=mesh, in_specs=in_specs, out_specs=out_specs, check_vma=False,
    )
```
